256 devices in a mesh: src: 32 (over y, z), tgt: 8 (over x, core).
Axes of the slice: x: 4, y: 4, z: 8, core: 2. Of those that a mesh axis runs over, the one named last changes fastest.
Arguments:
- source_points: bfloat16 [131072, 64], P('src'), may hold values from -4 to 4
- target_points: bfloat16 [262144, 64], P('tgt'), may hold values from -4 to 4
- tile_lists: int32 [512, 8, 4], P('src', 'tgt'), may hold values from 0 to 127, as said below
- tile_counts: int32 [512, 8], P('src', 'tgt'), may hold values from 1 to 4, as said below
Outputs:
- source_potential: float32 [131072], P('src')
- target_potential: float32 [262144], P('tgt')
The draws below stay inside these ranges and needn't reach their ends.
Inputs may be any that keep to these rules, and one draw needn't show every extreme that they name: `tile_lists`: the entries of one list are distinct; entries at slots k >= the count are valid numbers but not live; every target tile is live in some list. `tile_counts`: the largest count is 4 in every draw.
All inputs are finite; a program needn't handle non-finite values.
Results may differ from the reference program's by a relative error of at most 0.0003.
Values sent between devices are 32-bit elements; how exact they have to be, the bound alone decides.
No kernel may reach another device: no remote copies, remote signals or barrier semaphores. Data moves between devices by JAX's collectives and lax.ppermute only.
A program may use at most 128 MiB of HBM per device.

```python
import jax
import jax.numpy as jnp
from jax import lax

TILE = 256
E = 64
KLOC = 4
ITERS = 4
ST_DEV = 16
TT_DEV = 128
STILES = 512
NS = 131072
NT = 262144
N_SRC = 32
N_TGT = 8


def point_cloud(key, count):
    values = 0.5 * jax.random.normal(key, (count, E), jnp.float32)
    return jnp.clip(values, -4.0, 4.0).astype(jnp.bfloat16)


def draw_source_points(key, part):
    key = jax.random.fold_in(key, 3)
    return point_cloud(key, NS)


def draw_target_points(key, part):
    key = jax.random.fold_in(key, 4)
    return point_cloud(key, NT)


def draw_tile_lists(key, part):
    key = jax.random.fold_in(key, 11)
    rows = jnp.arange(STILES, dtype=jnp.int32)[:, None, None]
    shards = jnp.arange(N_TGT, dtype=jnp.int32)[None, :, None]
    slots = jnp.arange(KLOC, dtype=jnp.int32)[None, None, :]
    first = (rows + 7 * shards) % TT_DEV
    stride = jax.random.randint(key, (STILES, N_TGT, 1), 1, TT_DEV // KLOC + 1, jnp.int32)
    return ((first + slots * stride) % TT_DEV).astype(jnp.int32)


def draw_tile_counts(key, part):
    key = jax.random.fold_in(key, 5)
    load_key, count_key = jax.random.split(key)
    loads = jax.random.randint(load_key, (N_SRC,), max(KLOC // 2, 1), KLOC + 1, jnp.int32)
    row_loads = jnp.repeat(loads, ST_DEV)[:, None]
    counts = jax.random.randint(count_key, (STILES, N_TGT), 1, row_loads + 1, jnp.int32)
    return counts.at[0, 0].set(KLOC).astype(jnp.int32)


def setup_inputs(seed: int = 0) -> dict:
    splits = jax.random.split(jax.random.key(seed), 5)
    return {
        "source_points": draw_source_points(jax.random.fold_in(splits[4], 71), 0),
        "target_points": draw_target_points(jax.random.fold_in(splits[4], 71), 0),
        "tile_lists": draw_tile_lists(jax.random.fold_in(splits[4], 71), 0),
        "tile_counts": draw_tile_counts(jax.random.fold_in(splits[4], 71), 0),
    }


epsilon = 1.0
lowest = -1.0e30


def block_costs(tile_x, norm_x, tiles_y, norms_y):
    products = jnp.einsum("ie,bje->bij", tile_x.astype(jnp.float32), tiles_y.astype(jnp.float32))
    return norm_x[None, :, None] + norms_y[:, None, :] - products


def reference(source_points, target_points, tile_lists, tile_counts):
    source_count = NS // TILE
    target_count = NT // TILE
    source_tiles = source_points.reshape(source_count, TILE, E)
    target_tiles = target_points.reshape(target_count, TILE, E)
    source_norm = 0.5 * jnp.sum(jnp.square(source_tiles.astype(jnp.float32)), -1)
    target_norm = 0.5 * jnp.sum(jnp.square(target_tiles.astype(jnp.float32)), -1)
    offsets = (jnp.arange(N_TGT, dtype=jnp.int32) * TT_DEV)[None, :, None]
    global_lists = (tile_lists + offsets).astype(jnp.int32).reshape(source_count, N_TGT * KLOC)
    usable_all = (jnp.arange(KLOC, dtype=jnp.int32)[None, None, :] < tile_counts[:, :, None]).reshape(source_count, N_TGT * KLOC)
    log_source = -jnp.log(jnp.float32(NS))
    log_target = -jnp.log(jnp.float32(NT))

    def row_update(potential_g):
        grid_g = potential_g.reshape(target_count, TILE)

        def row_tile(items):
            tile_x, norm_x, indices, usable = items
            costs = block_costs(tile_x, norm_x, target_tiles[indices], target_norm[indices])
            scores = (grid_g[indices][:, None, :] - costs) / epsilon
            scores = jnp.where(usable[:, None, None], scores, lowest)
            peak = jnp.max(scores, axis=(0, 2))
            total = jnp.sum(jnp.exp(scores - peak[None, :, None]), axis=(0, 2))
            return epsilon * log_source - epsilon * (peak + jnp.log(total))

        return lax.map(row_tile, (source_tiles, source_norm, global_lists, usable_all)).reshape(NS)

    def column_update(potential_f):
        grid_f = potential_f.reshape(source_count, TILE)

        def online(carry, items):
            highest, masses = carry
            tile_x, norm_x, indices, usable, row_f = items
            costs = block_costs(tile_x, norm_x, target_tiles[indices], target_norm[indices])
            scores = (row_f[None, :, None] - costs) / epsilon
            block_peak = jnp.max(scores, axis=1)
            block_mass = jnp.sum(jnp.exp(scores - block_peak[:, None, :]), axis=1)
            block_peak = jnp.where(usable[:, None], block_peak, lowest)
            block_mass = jnp.where(usable[:, None], block_mass, 0.0)
            old_peak = highest[indices]
            old_mass = masses[indices]
            new_peak = jnp.maximum(old_peak, block_peak)
            new_mass = old_mass * jnp.exp(old_peak - new_peak) + block_mass * jnp.exp(block_peak - new_peak)
            return (highest.at[indices].set(new_peak), masses.at[indices].set(new_mass)), None

        start = (jnp.full((target_count, TILE), lowest, jnp.float32), jnp.zeros((target_count, TILE), jnp.float32))
        (highest, masses), _ = lax.scan(online, start, (source_tiles, source_norm, global_lists, usable_all, grid_f))
        return (epsilon * log_target - epsilon * (highest + jnp.log(masses))).reshape(NT)

    potential_g = jnp.zeros((NT,), jnp.float32)
    potential_f = jnp.zeros((NS,), jnp.float32)
    for iteration in range(ITERS):
        potential_f = row_update(potential_g)
        potential_g = column_update(potential_f)
    return potential_f, potential_g
```

```python
import functools
import math

import jax
import jax.numpy as jnp
from jax import lax
from jax.experimental import pallas as pl
from jax.experimental.pallas import tpu as pltpu
from jax.sharding import PartitionSpec as P

TILE = 256
HALF = 128
E = 64
KLOC = 4
ITERS = 4
LOWEST = -1e30
SHIFT = 32.0
LOG2E = math.log2(math.e)
LN2 = math.log(2.0)
CHUNK = 128
UNROLL = 4
LANES = (slice(0, HALF), slice(HALF, TILE))
VMEM_LIMIT = 12 * 1024 * 1024
RESIDENT = True


def held(x, space):
    return pltpu.with_memory_space_constraint(x, space) if RESIDENT else x


def like(shape, dtype=jnp.float32):
    return pltpu.VMEM(shape, dtype) if RESIDENT else jax.ShapeDtypeStruct(shape, dtype)


SPACE = {"s": pltpu.SMEM, "v": pltpu.VMEM, "k": pltpu.VMEM, "w": pltpu.VMEM, "a": pl.ANY, "h": pltpu.HBM}


def call(kernel, outs, out_specs, specs, args, scratch=(), name=None):
    specs_of = lambda letters: [pl.BlockSpec(memory_space=SPACE[s]) for s in letters]
    args = [held(arg, SPACE[spec]) if spec in "vkwh" else arg for spec, arg in zip(specs, args, strict=True)]
    keep = max(specs.find("k"), specs.find("w"))
    if keep >= 0:
        outs, out_specs = (*outs, like(args[keep].shape, args[keep].dtype)), out_specs + ("a" if "k" in specs else "v")
    return pl.pallas_call(
        kernel,
        out_shape=tuple(outs),
        in_specs=specs_of(specs),
        out_specs=tuple(specs_of(out_specs)),
        scratch_shapes=list(scratch),
        input_output_aliases={keep: len(outs) - 1} if keep >= 0 else {},
        compiler_params=pltpu.CompilerParams(vmem_limit_bytes=VMEM_LIMIT),
        name=name,
    )(*args)


class Codes:
    def __init__(self, held, codes, sem):
        self.copy = pltpu.make_async_copy(held, codes, sem.at[0])
        self.copy.start()
        self.codes = codes

    def ready(self):
        self.copy.wait()
        return self.codes


def for_blocks(codes, tiles, block):
    count = codes[codes.shape[0] - 1]

    def one(i):
        slot = lax.div(codes[i], tiles)
        block(slot, lax.div(slot, KLOC), codes[i] - slot * tiles)

    def several(i, _):
        for j in range(UNROLL):
            one(i * UNROLL + j)
        return 0

    def single(i, _):
        one(i)
        return 0

    groups = lax.div(count, UNROLL)
    lax.fori_loop(0, groups, several, 0)
    lax.fori_loop(groups * UNROLL, count, single, 0)


def place(t):
    return pl.ds(pl.multiple_of(t * TILE, TILE), TILE)


def spread_tiles(rows, tall):
    for p in range(tall.shape[0]):
        for h in range(2):
            row = rows[2 * p + h : 2 * p + h + 1, :]
            tall[p, LANES[h], :] = jnp.broadcast_to(row, (HALF, HALF)).T


def lane_join(tall, join):
    rows = []
    for p in range(tall.shape[0]):
        for h in range(2):
            rows.append(join(tall[p, LANES[h], :].T, axis=0, keepdims=True))
    return jnp.concatenate(rows, axis=0)


def fill(out, value):
    for d in range(out.shape[0]):
        out[d] = value


def total_of(parts):
    return functools.reduce(jnp.add, parts)


def parts_of(ref):
    return [ref[d] for d in range(ref.shape[0])]


def lse_of(parts):
    top = functools.reduce(jnp.maximum, parts)
    return top + jnp.log2(total_of([jnp.exp2(part - top) for part in parts]))


def product(a, b):
    return jnp.dot(a, b, preferred_element_type=jnp.float32)


def half_norms(points):
    wide = points.astype(jnp.float32)
    return 0.5 * jnp.sum(wide * wide, axis=0, keepdims=True)


def lane_rows(row):
    return jnp.concatenate([row[:, i : i + HALF] for i in range(0, row.shape[1], HALF)], axis=0)


def row_first_kernel(
    lists_in, counts_in, me, x, y, codes, out, inner, x_norms, share_norms, tx, ty, lists, counts, xs, top, mass, sems
):
    tiles, targets = xs.shape[0], ty.shape[1] // TILE
    pairs = ((lists_in, lists), (counts_in, counts), (x, tx), (y, ty))
    copies = [pltpu.make_async_copy(*pair, sems.at[i]) for i, pair in enumerate(pairs)]
    for copy in copies:
        copy.start()
    copies[0].wait()
    copies[1].wait()

    def listed(p, n):
        for k in range(KLOC):
            codes[n + k] = (p * KLOC + k) * targets + lists[k, p]
        return n + counts[p]

    codes[codes.shape[0] - 1] = lax.fori_loop(0, tiles, listed, 0)
    top[...] = jnp.full_like(top, LOWEST)
    mass[...] = jnp.zeros_like(mass)
    copies[2].wait()
    norms = []
    for p in range(tiles):
        points = tx[:, p * TILE : (p + 1) * TILE]
        norms.append(lane_rows(half_norms(points)))
        xs[p] = points.astype(jnp.float32).T.astype(jnp.bfloat16)
    x_norms[...] = jnp.concatenate(norms, axis=0)
    copies[3].wait()
    width = share_norms.shape[0] * HALF
    share_norms[...] = lane_rows(half_norms(ty[:, pl.ds(pl.multiple_of(me[0] * width, width), width)]))

    def block(slot, p, t):
        points = ty[:, place(t)]
        norms = half_norms(points) * LOG2E
        for r in range(0, TILE, CHUNK):
            rows = slice(r, r + CHUNK)
            scores = product(xs[p, rows, :], points) * LOG2E
            inner[slot, rows, :] = scores
            scores -= norms
            one, two = scores[:, LANES[0]], scores[:, LANES[1]]
            old = top[p, rows, :]
            new = jnp.maximum(old, jnp.maximum(one, two))
            top[p, rows, :] = new
            mass[p, rows, :] = mass[p, rows, :] * jnp.exp2(old - new) + (jnp.exp2(one - new) + jnp.exp2(two - new))

    for_blocks(codes, targets, block)
    lses = []
    for p in range(tiles):
        for h in range(2):
            tops, masses = top[p, LANES[h], :].T, mass[p, LANES[h], :].T
            peak = jnp.max(tops, axis=0, keepdims=True)
            lses.append(peak + jnp.log2(jnp.sum(masses * jnp.exp2(tops - peak), axis=0, keepdims=True)))
    fill(out, jnp.concatenate(lses, axis=0))


def both(tall):
    return jnp.concatenate([tall, tall], axis=1)


def col_first_kernel(log_ns, held_codes, inner, parts, u, out, _, peak, total, tall, codes, sem):
    blocks = Codes(held_codes, codes, sem)
    rows = -log_ns - lse_of(parts_of(parts))
    u[...] = rows
    peak[...] = jnp.full_like(peak, LOWEST)
    total[...] = jnp.zeros_like(total)
    spread_tiles(rows, tall)

    def block(slot, p, t):
        scores = inner[slot] + both(tall[p])
        old = peak[t]
        new = jnp.maximum(old, jnp.max(scores, axis=0, keepdims=True))
        mass = jnp.sum(jnp.exp2(scores - new), axis=0, keepdims=True)
        peak[t] = new
        total[t] = total[t] * jnp.exp2(old - new) + mass

    for_blocks(blocks.ready(), out.shape[0], block)
    masses = total[...]
    out[...] = jnp.where(masses > 0.0, peak[...] + jnp.log2(masses), LOWEST)


def plan_kernel(held_codes, inner, u, w, out, plan, tall, acc, codes, sem):
    blocks = Codes(held_codes, codes, sem)
    spread_tiles(u[...] + SHIFT, tall)
    acc[...] = jnp.zeros_like(acc)

    def block(slot, p, t):
        column = w[t]
        for r in range(0, TILE, CHUNK):
            rows = slice(r, r + CHUNK)
            part = jnp.exp2(inner[slot, rows, :] + both(tall[p, rows, :]) + column)
            plan[slot, rows, :] = part
            acc[p, rows, :] += part[:, LANES[0]] + part[:, LANES[1]]

    for_blocks(blocks.ready(), w.shape[0], block)
    fill(out, lane_join(acc, jnp.sum))


def row_kernel(held_codes, plan, b, out, _, acc, codes, sem):
    blocks = Codes(held_codes, codes, sem)
    acc[...] = jnp.zeros_like(acc)

    def block(slot, p, t):
        first, second = b[t, :, LANES[0]], b[t, :, LANES[1]]
        for r in range(0, TILE, CHUNK):
            rows = slice(r, r + CHUNK)
            acc[p, rows, :] += plan[slot, rows, LANES[0]] * first + plan[slot, rows, LANES[1]] * second

    for_blocks(blocks.ready(), b.shape[0], block)
    fill(out, lane_join(acc, jnp.sum))


def col_kernel(ns, last, held_codes, plan, parts, *refs):
    u, x_norms, out, f, _, acc, tall, codes, sem = refs if last else (None, None, refs[0], None, *refs[1:])
    blocks = Codes(held_codes, codes, sem)
    a = 1.0 / (ns * total_of(parts_of(parts)))
    spread_tiles(a, tall)
    if last:
        f[...] = (u[...] + (jnp.log2(a) + SHIFT)) * LN2 + x_norms[...]
    acc[...] = jnp.zeros_like(acc)

    def block(slot, p, t):
        sums = [[None] * 2, [None] * 2]
        for r in range(0, TILE, 8):
            factor = tall[p, r : r + 8, :]
            for h in range(2):
                term = plan[slot, r : r + 8, LANES[h]] * factor
                chain = (r // 8) % 2
                sums[h][chain] = term if sums[h][chain] is None else sums[h][chain] + term
        for h in range(2):
            acc[t, :, LANES[h]] += sums[h][0] + sums[h][1]

    for_blocks(blocks.ready(), out.shape[0], block)
    out[...] = jnp.sum(acc[...], axis=1, keepdims=True)


def join_first_kernel(log_nt, parts, w, out):
    w[...] = -log_nt - lse_of(parts_of(parts))
    fill(out, w[...])


def join_kernel(nt, parts, out):
    fill(out, 1.0 / (nt * total_of(parts_of(parts))))


def join_last_kernel(log_nt, parts, w, share_norms, out):
    fill(out, (w[...] + (-log_nt - jnp.log2(total_of(parts_of(parts))))) * LN2 + share_norms[...])


def trade_tgt(pieces):
    return lax.all_to_all(pieces, "tgt", 0, 0)


def trade_src(pieces):
    return lax.all_to_all(pieces, "src", 0, 0)


def iterate(x, y, lists, counts, me, ns, nt, n_src, n_tgt, trade_tgt, trade_src):
    st, tt = x.shape[0] // TILE, y.shape[0] // TILE
    shape = (2 * st, HALF)
    share = (2 * tt // n_src, HALF)
    plain = lambda *shape: jax.ShapeDtypeStruct(shape, jnp.float32)
    scratch = lambda *shape: pltpu.VMEM(shape, jnp.float32)
    row, rows, col, cell, cells = like(shape), like((n_tgt, *shape)), like((tt, 1, TILE)), like(share), like((n_src, *share))
    length = (st * KLOC // HALF + 1) * HALF
    codes = jax.ShapeDtypeStruct((length,), jnp.int32)
    fetch = (pltpu.SMEM((length,), jnp.int32), pltpu.SemaphoreType.DMA((1,)))
    tall, stats = scratch(st, TILE, HALF), scratch(tt, 1, TILE)
    log_ns, log_nt = math.log2(ns), math.log2(nt)
    pieces = lambda v: trade_src(v.reshape((n_src, *share)))
    whole = lambda v: trade_src(v).reshape(tt, 1, TILE)

    blocks = like((st * KLOC, TILE, TILE))
    codes, lse, inner, x_norms, share_norms = call(
        row_first_kernel,
        (codes, rows, blocks, row, cell),
        "svvvv",
        "hhshh",
        (lists.T, counts, me, x.T, y.T),
        (
            pltpu.VMEM((E, st * TILE), jnp.bfloat16),
            pltpu.VMEM((E, tt * TILE), jnp.bfloat16),
            pltpu.SMEM((KLOC, st), jnp.int32),
            pltpu.SMEM((st,), jnp.int32),
            pltpu.VMEM((st, TILE, E), jnp.bfloat16),
            tall,
            tall,
            pltpu.SemaphoreType.DMA((4,)),
        ),
        "row_first",
    )
    u, lse, inner = call(
        functools.partial(col_first_kernel, log_ns), (row, col), "vv", "vkv", (codes, inner, trade_tgt(lse)),
        (stats, stats, tall, *fetch), "col_first",
    )
    w, share_w = call(functools.partial(join_first_kernel, log_nt), (cell, cells), "vv", "v", (pieces(lse),), (), "join")
    mass, plan = call(plan_kernel, (rows,), "v", "vwvv", (codes, inner, u, whole(share_w)), (tall, tall, *fetch), "plan")
    for iteration in range(1, ITERS):
        last = iteration == ITERS - 1
        mass, *f, plan = call(
            functools.partial(col_kernel, ns, last), (col, plain(*shape)) if last else (col,), "vv" if last else "v",
            "vkvvv" if last else "vkv", (codes, plan, trade_tgt(mass)) + ((u, x_norms) if last else ()),
            (scratch(tt, 8, TILE), tall, *fetch), "col",
        )
        if last:
            break
        (b,) = call(functools.partial(join_kernel, nt), (cells,), "v", "v", (pieces(mass),), (), "join")
        mass, plan = call(row_kernel, (rows,), "v", "vkv", (codes, plan, whole(b)), (tall, *fetch), "row")
    (g,) = call(
        functools.partial(join_last_kernel, log_nt), (cells,), "v", "vvv", (pieces(mass), w, share_norms), (), "join"
    )
    return f[0].reshape(-1), trade_src(g).reshape(-1)


def local(source_points, target_points, tile_lists, tile_counts):
    n_src, n_tgt = lax.axis_size("src"), lax.axis_size("tgt")
    ns, nt = source_points.shape[0] * n_src, target_points.shape[0] * n_tgt
    me = lax.axis_index("src").astype(jnp.int32).reshape(1)
    return iterate(
        source_points, target_points, tile_lists[:, 0, :], tile_counts[:, 0], me, ns, nt, n_src, n_tgt, trade_tgt, trade_src
    )


def solution(mesh):
    in_specs = (P("src", None), P("tgt", None), P("src", "tgt", None), P("src", "tgt"))
    out_specs = (P("src"), P("tgt"))
    return jax.shard_map(local, mesh=mesh, in_specs=in_specs, out_specs=out_specs, check_vma=False)
```

```python
import functools
import math

import jax
import jax.numpy as jnp
from jax import lax
from jax.experimental import pallas as pl
from jax.experimental.pallas import tpu as pltpu
from jax.sharding import PartitionSpec as P

TILE = 256
HALF = 128
E = 64
KLOC = 4
ITERS = 4
LOWEST = -1e30
SHIFT = 32.0
LOG2E = math.log2(math.e)
LN2 = math.log(2.0)
SMALL = 2.0**-60
CHUNK = 128
LANES = (slice(0, HALF), slice(HALF, TILE))
VMEM_LIMIT = 12 * 1024 * 1024
RESIDENT = True


def held(x, space):
    return pltpu.with_memory_space_constraint(x, space) if RESIDENT else x


def like(shape, dtype=jnp.float32):
    return pltpu.VMEM(shape, dtype) if RESIDENT else jax.ShapeDtypeStruct(shape, dtype)


SPACE = {"s": pltpu.SMEM, "v": pltpu.VMEM, "k": pltpu.VMEM, "w": pltpu.VMEM, "a": pl.ANY, "h": pltpu.HBM}


def call(kernel, outs, out_specs, specs, args, scratch=(), name=None):
    specs_of = lambda letters: [pl.BlockSpec(memory_space=SPACE[s]) for s in letters]
    args = [held(arg, SPACE[spec]) if spec in "vkwh" else arg for spec, arg in zip(specs, args, strict=True)]
    keep = max(specs.find("k"), specs.find("w"))
    if keep >= 0:
        outs, out_specs = (*outs, like(args[keep].shape, args[keep].dtype)), out_specs + ("a" if "k" in specs else "v")
    return pl.pallas_call(
        kernel,
        out_shape=tuple(outs),
        in_specs=specs_of(specs),
        out_specs=tuple(specs_of(out_specs)),
        scratch_shapes=list(scratch),
        input_output_aliases={keep: len(outs) - 1} if keep >= 0 else {},
        compiler_params=pltpu.CompilerParams(vmem_limit_bytes=VMEM_LIMIT),
        name=name,
    )(*args)


class Codes:
    def __init__(self, held, codes, sem):
        self.copy = pltpu.make_async_copy(held, codes, sem.at[0])
        self.copy.start()
        self.codes = codes

    def ready(self):
        self.copy.wait()
        return self.codes


def for_blocks(codes, tiles, block, unroll=4):
    count = codes[codes.shape[0] - 1]

    def one(i):
        slot = lax.div(codes[i], tiles)
        block(slot, lax.div(slot, KLOC), codes[i] - slot * tiles)

    def several(i, _):
        for j in range(unroll):
            one(i * unroll + j)
        return 0

    def single(i, _):
        one(i)
        return 0

    groups = lax.div(count, unroll)
    lax.fori_loop(0, groups, several, 0)
    lax.fori_loop(groups * unroll, count, single, 0)


def place(t):
    return pl.ds(pl.multiple_of(t * TILE, TILE), TILE)


def spread_tiles(rows, tall):
    for p in range(tall.shape[0]):
        for h in range(2):
            row = rows[2 * p + h : 2 * p + h + 1, :]
            tall[p, LANES[h], :] = jnp.broadcast_to(row, (HALF, HALF)).T


def lane_join(tall, join):
    rows = []
    for p in range(tall.shape[0]):
        for h in range(2):
            rows.append(join(tall[p, LANES[h], :].T, axis=0, keepdims=True))
    return jnp.concatenate(rows, axis=0)


def fill(out, value):
    for d in range(out.shape[0]):
        out[d] = value


def total_of(parts):
    return functools.reduce(jnp.add, parts)


def parts_of(ref):
    return [ref[d] for d in range(ref.shape[0])]


def lse_of(parts):
    top = functools.reduce(jnp.maximum, parts)
    return top + jnp.log2(total_of([jnp.exp2(part - top) for part in parts]))


def product(a, b):
    return jnp.dot(a, b, preferred_element_type=jnp.float32)


def half_norms(points):
    wide = points.astype(jnp.float32)
    return 0.5 * jnp.sum(wide * wide, axis=0, keepdims=True)


def lane_rows(row):
    return jnp.concatenate([row[:, i : i + HALF] for i in range(0, row.shape[1], HALF)], axis=0)


def row_first_kernel(lists_in, counts_in, x, y, codes, out, costs, tx, ty, lists, counts, xs, tall, mass, sems):
    tiles, targets = xs.shape[0], ty.shape[1] // TILE
    pairs = ((lists_in, lists), (counts_in, counts), (x, tx), (y, ty))
    copies = [pltpu.make_async_copy(*pair, sems.at[i]) for i, pair in enumerate(pairs)]
    for copy in copies:
        copy.start()
    copies[0].wait()
    copies[1].wait()

    def listed(p, n):
        for k in range(KLOC):
            codes[n + k] = (p * KLOC + k) * targets + lists[k, p]
        return n + counts[p]

    codes[codes.shape[0] - 1] = lax.fori_loop(0, tiles, listed, 0)
    mass[...] = jnp.zeros_like(mass)
    copies[2].wait()
    norms = []
    for p in range(tiles):
        points = tx[:, p * TILE : (p + 1) * TILE]
        norms.append(lane_rows(half_norms(points)))
        xs[p] = points.astype(jnp.float32).T.astype(jnp.bfloat16)
    spread_tiles(jnp.concatenate(norms, axis=0) * LOG2E, tall)
    copies[3].wait()

    def block(slot, p, t):
        points = ty[:, place(t)]
        norms = half_norms(points) * LOG2E
        for r in range(0, TILE, CHUNK):
            rows = slice(r, r + CHUNK)
            scores = (product(xs[p, rows, :], points) * LOG2E - norms) - both(tall[p, rows, :])
            costs[slot, rows, :] = scores
            terms = jnp.exp2(scores)
            mass[p, rows, :] += terms[:, LANES[0]] + terms[:, LANES[1]]

    for_blocks(codes, targets, block, 8)
    sums = lane_join(mass, jnp.sum)
    fill(out, jnp.log2(sums))

    @pl.when(jnp.min(sums) < SMALL)
    def _():
        top = tall
        top[...] = jnp.full_like(top, LOWEST)
        mass[...] = jnp.zeros_like(mass)

        def again(slot, p, t):
            one, two = costs[slot, :, LANES[0]], costs[slot, :, LANES[1]]
            old = top[p]
            new = jnp.maximum(old, jnp.maximum(one, two))
            top[p] = new
            mass[p] = mass[p] * jnp.exp2(old - new) + (jnp.exp2(one - new) + jnp.exp2(two - new))

        for_blocks(codes, targets, again, 1)
        lses = []
        for p in range(tiles):
            for h in range(2):
                tops, masses = top[p, LANES[h], :].T, mass[p, LANES[h], :].T
                peak = jnp.max(tops, axis=0, keepdims=True)
                lses.append(peak + jnp.log2(jnp.sum(masses * jnp.exp2(tops - peak), axis=0, keepdims=True)))
        fill(out, jnp.concatenate(lses, axis=0))


def both(tall):
    return jnp.concatenate([tall, tall], axis=1)


def col_first_kernel(log_ns, held_codes, costs, parts, f, out, peaks, terms, peak, total, tall, codes, sem):
    blocks = Codes(held_codes, codes, sem)
    rows = -log_ns - lse_of(parts_of(parts))
    f[...] = rows
    peak[...] = jnp.full_like(peak, LOWEST)
    total[...] = jnp.zeros_like(total)
    spread_tiles(rows, tall)

    def block(slot, p, t):
        scores = costs[slot] + both(tall[p])
        old = peak[t]
        new = jnp.maximum(old, jnp.max(scores, axis=0, keepdims=True))
        part = jnp.exp2(scores - new)
        terms[slot] = part
        peaks[slot] = new
        peak[t] = new
        total[t] = total[t] * jnp.exp2(old - new) + jnp.sum(part, axis=0, keepdims=True)

    for_blocks(blocks.ready(), out.shape[0], block)
    masses = total[...]
    out[...] = jnp.where(masses > 0.0, peak[...] + jnp.log2(masses), LOWEST)


def row_kernel(first, held_codes, terms, b, given, out, *refs):
    made, _, acc, codes, sem = refs if first else (None, *refs)
    blocks = Codes(held_codes, codes, sem)
    acc[...] = jnp.zeros_like(acc)

    def block(slot, p, t):
        if first:
            factor = jnp.exp2(given[slot] + (b[t] + SHIFT))
            made[slot] = factor
        else:
            factor = given[slot] * b[t]
        for r in range(0, TILE, CHUNK):
            rows = slice(r, r + CHUNK)
            acc[p, rows, :] += (
                terms[slot, rows, LANES[0]] * factor[:, LANES[0]] + terms[slot, rows, LANES[1]] * factor[:, LANES[1]]
            )

    for_blocks(blocks.ready(), b.shape[0], block)
    fill(out, lane_join(acc, jnp.sum))


def col_kernel(ns, last, held_codes, terms, parts, factors, *refs):
    first, out, f, _, acc, tall, codes, sem = refs if last else (None, refs[0], None, *refs[1:])
    blocks = Codes(held_codes, codes, sem)
    a = 1.0 / (ns * total_of(parts_of(parts)))
    spread_tiles(a, tall)
    if last:
        f[...] = (first[...] + (jnp.log2(a) + SHIFT)) * LN2
    acc[...] = jnp.zeros_like(acc)

    def block(slot, p, t):
        sums = [[None] * 2, [None] * 2]
        for r in range(0, TILE, 8):
            factor = tall[p, r : r + 8, :]
            for h in range(2):
                term = terms[slot, r : r + 8, LANES[h]] * factor
                chain = (r // 8) % 2
                sums[h][chain] = term if sums[h][chain] is None else sums[h][chain] + term
        for h in range(2):
            acc[t, :, LANES[h]] += (sums[h][0] + sums[h][1]) * factors[slot, :, LANES[h]]

    for_blocks(blocks.ready(), out.shape[0], block)
    out[...] = jnp.sum(acc[...], axis=1, keepdims=True)


def join_first_kernel(log_nt, parts, g, out):
    g[...] = -log_nt - lse_of(parts_of(parts))
    fill(out, g[...])


def join_kernel(nt, parts, out):
    fill(out, 1.0 / (nt * total_of(parts_of(parts))))


def join_last_kernel(log_nt, parts, g, out):
    fill(out, (g[...] + (-log_nt - jnp.log2(total_of(parts_of(parts))))) * LN2)


def trade_tgt(pieces):
    return lax.all_to_all(pieces, "tgt", 0, 0)


def trade_src(pieces):
    return lax.all_to_all(pieces, "src", 0, 0)


def iterate(x, y, lists, counts, ns, nt, n_src, n_tgt, trade_tgt, trade_src):
    st, tt = x.shape[0] // TILE, y.shape[0] // TILE
    shape = (2 * st, HALF)
    share = (2 * tt // n_src, HALF)
    plain = lambda *shape: jax.ShapeDtypeStruct(shape, jnp.float32)
    scratch = lambda *shape: pltpu.VMEM(shape, jnp.float32)
    row, rows, col, cell, cells = like(shape), like((n_tgt, *shape)), like((tt, 1, TILE)), like(share), like((n_src, *share))
    length = (st * KLOC // HALF + 1) * HALF
    codes = jax.ShapeDtypeStruct((length,), jnp.int32)
    fetch = (pltpu.SMEM((length,), jnp.int32), pltpu.SemaphoreType.DMA((1,)))
    tall, stats = scratch(st, TILE, HALF), scratch(tt, 1, TILE)
    log_ns, log_nt = math.log2(ns), math.log2(nt)
    pieces = lambda v: trade_src(v.reshape((n_src, *share)))
    whole = lambda v: trade_src(v).reshape(tt, 1, TILE)

    blocks = like((st * KLOC, TILE, TILE))
    codes, lse, costs = call(
        row_first_kernel,
        (codes, rows, blocks),
        "svv",
        "hhhh",
        (lists.T, counts, x.T, y.T),
        (
            pltpu.VMEM((E, st * TILE), jnp.bfloat16),
            pltpu.VMEM((E, tt * TILE), jnp.bfloat16),
            pltpu.SMEM((KLOC, st), jnp.int32),
            pltpu.SMEM((st,), jnp.int32),
            pltpu.VMEM((st, TILE, E), jnp.bfloat16),
            tall,
            tall,
            pltpu.SemaphoreType.DMA((4,)),
        ),
        "row_first",
    )
    each = like((st * KLOC, 1, TILE))
    first, lse, peaks, terms = call(
        functools.partial(col_first_kernel, log_ns), (row, col, each, blocks), "vvvv", "vvv", (codes, costs, trade_tgt(lse)),
        (stats, stats, tall, *fetch), "col_first",
    )
    g, share_g = call(functools.partial(join_first_kernel, log_nt), (cell, cells), "vv", "v", (pieces(lse),), (), "join")
    mass, factors, terms = call(
        functools.partial(row_kernel, True), (rows, each), "vv", "vkvv", (codes, terms, whole(share_g), peaks),
        (tall, *fetch), "row_second",
    )
    for iteration in range(1, ITERS):
        last = iteration == ITERS - 1
        mass, *f, terms = call(
            functools.partial(col_kernel, ns, last), (col, plain(*shape)) if last else (col,), "vv" if last else "v",
            "vkvvv" if last else "vkvv", (codes, terms, trade_tgt(mass), factors) + ((first,) if last else ()),
            (scratch(tt, 8, TILE), tall, *fetch), "col",
        )
        if last:
            break
        (b,) = call(functools.partial(join_kernel, nt), (cells,), "v", "v", (pieces(mass),), (), "join")
        mass, terms = call(
            functools.partial(row_kernel, False), (rows,), "v", "vkvv", (codes, terms, whole(b), factors),
            (tall, *fetch), "row",
        )
    (share_g,) = call(functools.partial(join_last_kernel, log_nt), (cells,), "v", "vv", (pieces(mass), g), (), "join")
    return f[0].reshape(-1), trade_src(share_g).reshape(-1)


def local(source_points, target_points, tile_lists, tile_counts):
    n_src, n_tgt = lax.axis_size("src"), lax.axis_size("tgt")
    ns, nt = source_points.shape[0] * n_src, target_points.shape[0] * n_tgt
    return iterate(
        source_points, target_points, tile_lists[:, 0, :], tile_counts[:, 0], ns, nt, n_src, n_tgt, trade_tgt, trade_src
    )


def solution(mesh):
    in_specs = (P("src", None), P("tgt", None), P("src", "tgt", None), P("src", "tgt"))
    out_specs = (P("src"), P("tgt"))
    return jax.shard_map(local, mesh=mesh, in_specs=in_specs, out_specs=out_specs, check_vma=False)
```

```python
import functools
import math

import jax
import jax.numpy as jnp
from jax import lax
from jax.experimental import pallas as pl
from jax.experimental.pallas import tpu as pltpu
from jax.sharding import PartitionSpec as P

TILE = 256
HALF = 128
E = 64
KLOC = 4
ITERS = 4
LOWEST = -1e30
SHIFT = 32.0
LOG2E = math.log2(math.e)
LN2 = math.log(2.0)
SMALL = 2.0**-60
CHUNK = 128
LANES = (slice(0, HALF), slice(HALF, TILE))
VMEM_LIMIT = 12 * 1024 * 1024
RESIDENT = True


def held(x, space):
    return pltpu.with_memory_space_constraint(x, space) if RESIDENT else x


def like(shape, dtype=jnp.float32):
    return pltpu.VMEM(shape, dtype) if RESIDENT else jax.ShapeDtypeStruct(shape, dtype)


SPACE = {"s": pltpu.SMEM, "v": pltpu.VMEM, "k": pltpu.VMEM, "w": pltpu.VMEM, "a": pl.ANY, "h": pltpu.HBM}


def call(kernel, outs, out_specs, specs, args, scratch=(), name=None):
    specs_of = lambda letters: [pl.BlockSpec(memory_space=SPACE[s]) for s in letters]
    args = [held(arg, SPACE[spec]) if spec in "vkwh" else arg for spec, arg in zip(specs, args, strict=True)]
    keep = max(specs.find("k"), specs.find("w"))
    if keep >= 0:
        outs, out_specs = (*outs, like(args[keep].shape, args[keep].dtype)), out_specs + ("a" if "k" in specs else "v")
    return pl.pallas_call(
        kernel,
        out_shape=tuple(outs),
        in_specs=specs_of(specs),
        out_specs=tuple(specs_of(out_specs)),
        scratch_shapes=list(scratch),
        input_output_aliases={keep: len(outs) - 1} if keep >= 0 else {},
        compiler_params=pltpu.CompilerParams(vmem_limit_bytes=VMEM_LIMIT),
        name=name,
    )(*args)


class Codes:
    def __init__(self, held, codes, sem):
        self.copy = pltpu.make_async_copy(held, codes, sem.at[0])
        self.copy.start()
        self.codes = codes

    def ready(self):
        self.copy.wait()
        return self.codes


def for_blocks(codes, tiles, block, unroll=4):
    count = codes[codes.shape[0] - 1]

    def one(i):
        slot = lax.div(codes[i], tiles)
        block(slot, lax.div(slot, KLOC), codes[i] - slot * tiles)

    def several(i, _):
        for j in range(unroll):
            one(i * unroll + j)
        return 0

    def single(i, _):
        one(i)
        return 0

    groups = lax.div(count, unroll)
    lax.fori_loop(0, groups, several, 0)
    lax.fori_loop(groups * unroll, count, single, 0)


def place(t):
    return pl.ds(pl.multiple_of(t * TILE, TILE), TILE)


def spread_tiles(rows, tall):
    for p in range(tall.shape[0]):
        for h in range(2):
            row = rows[2 * p + h : 2 * p + h + 1, :]
            tall[p, LANES[h], :] = jnp.broadcast_to(row, (HALF, HALF)).T


def lane_join(tall, join):
    rows = []
    for p in range(tall.shape[0]):
        for h in range(2):
            rows.append(join(tall[p, LANES[h], :].T, axis=0, keepdims=True))
    return jnp.concatenate(rows, axis=0)


def fill(out, value):
    for d in range(out.shape[0]):
        out[d] = value


def total_of(parts):
    return functools.reduce(jnp.add, parts)


def parts_of(ref):
    return [ref[d] for d in range(ref.shape[0])]


def lse_of(parts):
    top = functools.reduce(jnp.maximum, parts)
    return top + jnp.log2(total_of([jnp.exp2(part - top) for part in parts]))


def product(a, b):
    return jnp.dot(a, b, preferred_element_type=jnp.float32)


def half_norms(points):
    wide = points.astype(jnp.float32)
    return 0.5 * jnp.sum(wide * wide, axis=0, keepdims=True)


def lane_rows(row):
    return jnp.concatenate([row[:, i : i + HALF] for i in range(0, row.shape[1], HALF)], axis=0)


def row_first_kernel(lists_in, counts_in, x, y, codes, out, costs, tx, ty, lists, counts, xs, tall, mass, sems):
    tiles, targets = xs.shape[0], ty.shape[1] // TILE
    pairs = ((lists_in, lists), (counts_in, counts), (x, tx), (y, ty))
    copies = [pltpu.make_async_copy(*pair, sems.at[i]) for i, pair in enumerate(pairs)]
    for copy in copies:
        copy.start()
    copies[0].wait()
    copies[1].wait()

    def listed(p, n):
        for k in range(KLOC):
            codes[n + k] = (p * KLOC + k) * targets + lists[k, p]
        return n + counts[p]

    codes[codes.shape[0] - 1] = lax.fori_loop(0, tiles, listed, 0)
    mass[...] = jnp.zeros_like(mass)
    copies[2].wait()
    norms = []
    for p in range(tiles):
        points = tx[:, p * TILE : (p + 1) * TILE]
        norms.append(lane_rows(half_norms(points)))
        xs[p] = points.astype(jnp.float32).T.astype(jnp.bfloat16)
    spread_tiles(jnp.concatenate(norms, axis=0) * LOG2E, tall)
    copies[3].wait()

    def block(slot, p, t):
        points = ty[:, place(t)]
        norms = half_norms(points) * LOG2E
        for r in range(0, TILE, CHUNK):
            rows = slice(r, r + CHUNK)
            scores = (product(xs[p, rows, :], points) * LOG2E - norms) - both(tall[p, rows, :])
            costs[slot, rows, :] = scores
            terms = jnp.exp2(scores)
            mass[p, rows, :] += terms[:, LANES[0]] + terms[:, LANES[1]]

    for_blocks(codes, targets, block, 8)
    sums = lane_join(mass, jnp.sum)
    fill(out, jnp.log2(sums))

    @pl.when(jnp.min(sums) < SMALL)
    def _():
        top = tall
        top[...] = jnp.full_like(top, LOWEST)
        mass[...] = jnp.zeros_like(mass)

        def again(slot, p, t):
            one, two = costs[slot, :, LANES[0]], costs[slot, :, LANES[1]]
            old = top[p]
            new = jnp.maximum(old, jnp.maximum(one, two))
            top[p] = new
            mass[p] = mass[p] * jnp.exp2(old - new) + (jnp.exp2(one - new) + jnp.exp2(two - new))

        for_blocks(codes, targets, again, 1)
        lses = []
        for p in range(tiles):
            for h in range(2):
                tops, masses = top[p, LANES[h], :].T, mass[p, LANES[h], :].T
                peak = jnp.max(tops, axis=0, keepdims=True)
                lses.append(peak + jnp.log2(jnp.sum(masses * jnp.exp2(tops - peak), axis=0, keepdims=True)))
        fill(out, jnp.concatenate(lses, axis=0))


def both(tall):
    return jnp.concatenate([tall, tall], axis=1)


def col_first_kernel(log_ns, held_codes, costs, parts, f, out, peaks, terms, peak, total, tall, codes, sem):
    blocks = Codes(held_codes, codes, sem)
    rows = -log_ns - lse_of(parts_of(parts))
    f[...] = rows
    peak[...] = jnp.full_like(peak, LOWEST)
    total[...] = jnp.zeros_like(total)
    spread_tiles(rows, tall)

    def block(slot, p, t):
        scores = costs[slot] + both(tall[p])
        old = peak[t]
        new = jnp.maximum(old, jnp.max(scores, axis=0, keepdims=True))
        part = jnp.exp2(scores - new)
        terms[slot] = part
        peaks[slot] = new
        peak[t] = new
        total[t] = total[t] * jnp.exp2(old - new) + jnp.sum(part, axis=0, keepdims=True)

    for_blocks(blocks.ready(), out.shape[0], block)
    masses = total[...]
    out[...] = jnp.where(masses > 0.0, peak[...] + jnp.log2(masses), LOWEST)


def row_kernel(first, held_codes, terms, b, given, out, *refs):
    made, _, acc, codes, sem = refs if first else (None, *refs)
    blocks = Codes(held_codes, codes, sem)
    acc[...] = jnp.zeros_like(acc)

    def block(slot, p, t):
        if first:
            factor = jnp.exp2(given[slot] + (b[t] + SHIFT))
            made[slot] = factor
        else:
            factor = given[slot] * b[t]
        for r in range(0, TILE, CHUNK):
            rows = slice(r, r + CHUNK)
            acc[p, rows, :] += (
                terms[slot, rows, LANES[0]] * factor[:, LANES[0]] + terms[slot, rows, LANES[1]] * factor[:, LANES[1]]
            )

    for_blocks(blocks.ready(), b.shape[0], block)
    fill(out, lane_join(acc, jnp.sum))


def col_kernel(ns, last, held_codes, terms, parts, factors, *refs):
    first, out, f, _, acc, tall, codes, sem = refs if last else (None, refs[0], None, *refs[1:])
    blocks = Codes(held_codes, codes, sem)
    a = 1.0 / (ns * total_of(parts_of(parts)))
    spread_tiles(a, tall)
    if last:
        f[...] = (first[...] + (jnp.log2(a) + SHIFT)) * LN2
    acc[...] = jnp.zeros_like(acc)

    def block(slot, p, t):
        sums = [[None] * 2, [None] * 2]
        for r in range(0, TILE, 8):
            factor = tall[p, r : r + 8, :]
            for h in range(2):
                term = terms[slot, r : r + 8, LANES[h]] * factor
                chain = (r // 8) % 2
                sums[h][chain] = term if sums[h][chain] is None else sums[h][chain] + term
        for h in range(2):
            acc[t, :, LANES[h]] += (sums[h][0] + sums[h][1]) * factors[slot, :, LANES[h]]

    for_blocks(blocks.ready(), out.shape[0], block)
    out[...] = jnp.sum(acc[...], axis=1, keepdims=True)


def join_first_kernel(log_nt, parts, g, out):
    g[...] = -log_nt - lse_of(parts_of(parts))
    fill(out, g[...])


def join_kernel(nt, parts, out):
    fill(out, 1.0 / (nt * total_of(parts_of(parts))))


def join_last_kernel(log_nt, parts, g, out):
    fill(out, (g[...] + (-log_nt - jnp.log2(total_of(parts_of(parts))))) * LN2)


def trade_tgt(pieces):
    return lax.all_to_all(pieces, "tgt", 0, 0)


def trade_src(pieces):
    order = [y * 8 + z for z in range(8) for y in range(4)]
    return lax.all_to_all(pieces, "src", 0, 0, axis_index_groups=[order])


def iterate(x, y, lists, counts, ns, nt, n_src, n_tgt, trade_tgt, trade_src):
    st, tt = x.shape[0] // TILE, y.shape[0] // TILE
    shape = (2 * st, HALF)
    share = (2 * tt // n_src, HALF)
    plain = lambda *shape: jax.ShapeDtypeStruct(shape, jnp.float32)
    scratch = lambda *shape: pltpu.VMEM(shape, jnp.float32)
    row, rows, col, cell, cells = like(shape), like((n_tgt, *shape)), like((tt, 1, TILE)), like(share), like((n_src, *share))
    length = (st * KLOC // HALF + 1) * HALF
    codes = jax.ShapeDtypeStruct((length,), jnp.int32)
    fetch = (pltpu.SMEM((length,), jnp.int32), pltpu.SemaphoreType.DMA((1,)))
    tall, stats = scratch(st, TILE, HALF), scratch(tt, 1, TILE)
    log_ns, log_nt = math.log2(ns), math.log2(nt)
    pieces = lambda v: trade_src(v.reshape((n_src, *share)))
    whole = lambda v: trade_src(v).reshape(tt, 1, TILE)

    blocks = like((st * KLOC, TILE, TILE))
    codes, lse, costs = call(
        row_first_kernel,
        (codes, rows, blocks),
        "svv",
        "hhhh",
        (lists.T, counts, x.T, y.T),
        (
            pltpu.VMEM((E, st * TILE), jnp.bfloat16),
            pltpu.VMEM((E, tt * TILE), jnp.bfloat16),
            pltpu.SMEM((KLOC, st), jnp.int32),
            pltpu.SMEM((st,), jnp.int32),
            pltpu.VMEM((st, TILE, E), jnp.bfloat16),
            tall,
            tall,
            pltpu.SemaphoreType.DMA((4,)),
        ),
        "row_first",
    )
    each = like((st * KLOC, 1, TILE))
    first, lse, peaks, terms = call(
        functools.partial(col_first_kernel, log_ns), (row, col, each, blocks), "vvvv", "vvv", (codes, costs, trade_tgt(lse)),
        (stats, stats, tall, *fetch), "col_first",
    )
    g, share_g = call(functools.partial(join_first_kernel, log_nt), (cell, cells), "vv", "v", (pieces(lse),), (), "join")
    mass, factors, terms = call(
        functools.partial(row_kernel, True), (rows, each), "vv", "vkvv", (codes, terms, whole(share_g), peaks),
        (tall, *fetch), "row_second",
    )
    for iteration in range(1, ITERS):
        last = iteration == ITERS - 1
        mass, *f, terms = call(
            functools.partial(col_kernel, ns, last), (col, plain(*shape)) if last else (col,), "vv" if last else "v",
            "vkvvv" if last else "vkvv", (codes, terms, trade_tgt(mass), factors) + ((first,) if last else ()),
            (scratch(tt, 8, TILE), tall, *fetch), "col",
        )
        if last:
            break
        (b,) = call(functools.partial(join_kernel, nt), (cells,), "v", "v", (pieces(mass),), (), "join")
        mass, terms = call(
            functools.partial(row_kernel, False), (rows,), "v", "vkvv", (codes, terms, whole(b), factors),
            (tall, *fetch), "row",
        )
    (share_g,) = call(functools.partial(join_last_kernel, log_nt), (cells,), "v", "vv", (pieces(mass), g), (), "join")
    return f[0].reshape(-1), trade_src(share_g).reshape(-1)


def local(source_points, target_points, tile_lists, tile_counts):
    n_src, n_tgt = lax.axis_size("src"), lax.axis_size("tgt")
    ns, nt = source_points.shape[0] * n_src, target_points.shape[0] * n_tgt
    return iterate(
        source_points, target_points, tile_lists[:, 0, :], tile_counts[:, 0], ns, nt, n_src, n_tgt, trade_tgt, trade_src
    )


def solution(mesh):
    in_specs = (P("src", None), P("tgt", None), P("src", "tgt", None), P("src", "tgt"))
    out_specs = (P("src"), P("tgt"))
    return jax.shard_map(local, mesh=mesh, in_specs=in_specs, out_specs=out_specs, check_vma=False)
```

```python
import functools
import math

import jax
import jax.numpy as jnp
from jax import lax
from jax.experimental import pallas as pl
from jax.experimental.pallas import tpu as pltpu
from jax.sharding import PartitionSpec as P

TILE = 256
HALF = 128
E = 64
KLOC = 4
ITERS = 4
LOWEST = -1e30
SHIFT = 32.0
LOG2E = math.log2(math.e)
LN2 = math.log(2.0)
SMALL = 2.0**-60
CHUNK = 128
LANES = (slice(0, HALF), slice(HALF, TILE))
VMEM_LIMIT = 12 * 1024 * 1024
RESIDENT = True


def held(x, space):
    return pltpu.with_memory_space_constraint(x, space) if RESIDENT else x


def like(shape, dtype=jnp.float32):
    return pltpu.VMEM(shape, dtype) if RESIDENT else jax.ShapeDtypeStruct(shape, dtype)


SPACE = {"s": pltpu.SMEM, "v": pltpu.VMEM, "k": pltpu.VMEM, "w": pltpu.VMEM, "a": pl.ANY, "h": pltpu.HBM}


def call(kernel, outs, out_specs, specs, args, scratch=(), name=None):
    specs_of = lambda letters: [pl.BlockSpec(memory_space=SPACE[s]) for s in letters]
    args = [held(arg, SPACE[spec]) if spec in "vkwh" else arg for spec, arg in zip(specs, args, strict=True)]
    keep = max(specs.find("k"), specs.find("w"))
    if keep >= 0:
        outs, out_specs = (*outs, like(args[keep].shape, args[keep].dtype)), out_specs + ("a" if "k" in specs else "v")
    return pl.pallas_call(
        kernel,
        out_shape=tuple(outs),
        in_specs=specs_of(specs),
        out_specs=tuple(specs_of(out_specs)),
        scratch_shapes=list(scratch),
        input_output_aliases={keep: len(outs) - 1} if keep >= 0 else {},
        compiler_params=pltpu.CompilerParams(vmem_limit_bytes=VMEM_LIMIT),
        name=name,
    )(*args)


class Codes:
    def __init__(self, held, codes, sem):
        self.copy = pltpu.make_async_copy(held, codes, sem.at[0])
        self.copy.start()
        self.codes = codes

    def ready(self):
        self.copy.wait()
        return self.codes


def for_blocks(codes, tiles, block, unroll=4):
    count = codes[codes.shape[0] - 1]

    def one(i):
        slot = lax.div(codes[i], tiles)
        block(slot, lax.div(slot, KLOC), codes[i] - slot * tiles)

    def several(i, _):
        for j in range(unroll):
            one(i * unroll + j)
        return 0

    def single(i, _):
        one(i)
        return 0

    groups = lax.div(count, unroll)
    lax.fori_loop(0, groups, several, 0)
    lax.fori_loop(groups * unroll, count, single, 0)


def place(t):
    return pl.ds(pl.multiple_of(t * TILE, TILE), TILE)


def spread_tiles(rows, tall):
    for p in range(tall.shape[0]):
        for h in range(2):
            row = rows[2 * p + h : 2 * p + h + 1, :]
            tall[p, LANES[h], :] = jnp.broadcast_to(row, (HALF, HALF)).T


def lane_join(tall, join):
    rows = []
    for p in range(tall.shape[0]):
        for h in range(2):
            rows.append(join(tall[p, LANES[h], :].T, axis=0, keepdims=True))
    return jnp.concatenate(rows, axis=0)


def fill(out, value):
    for d in range(out.shape[0]):
        out[d] = value


def total_of(parts):
    return functools.reduce(jnp.add, parts)


def parts_of(ref):
    return [ref[d] for d in range(ref.shape[0])]


def lse_of(parts):
    top = functools.reduce(jnp.maximum, parts)
    return top + jnp.log2(total_of([jnp.exp2(part - top) for part in parts]))


def product(a, b):
    return jnp.dot(a, b, preferred_element_type=jnp.float32)


def half_norms(points):
    wide = points.astype(jnp.float32)
    return 0.5 * jnp.sum(wide * wide, axis=0, keepdims=True)


def lane_rows(row):
    return jnp.concatenate([row[:, i : i + HALF] for i in range(0, row.shape[1], HALF)], axis=0)


def row_first_kernel(lists_in, counts_in, x, y, codes, out, costs, tx, ty, lists, counts, xs, tall, mass, sems):
    tiles, targets = xs.shape[0], ty.shape[1] // TILE
    pairs = ((lists_in, lists), (counts_in, counts), (x, tx), (y, ty))
    copies = [pltpu.make_async_copy(*pair, sems.at[i]) for i, pair in enumerate(pairs)]
    for copy in copies:
        copy.start()
    copies[0].wait()
    copies[1].wait()

    def listed(p, n):
        for k in range(KLOC):
            codes[n + k] = (p * KLOC + k) * targets + lists[k, p]
        return n + counts[p]

    codes[codes.shape[0] - 1] = lax.fori_loop(0, tiles, listed, 0)
    mass[...] = jnp.zeros_like(mass)
    copies[2].wait()
    norms = []
    for p in range(tiles):
        points = tx[:, p * TILE : (p + 1) * TILE]
        norms.append(lane_rows(half_norms(points)))
        xs[p] = points.astype(jnp.float32).T.astype(jnp.bfloat16)
    spread_tiles(jnp.concatenate(norms, axis=0) * LOG2E, tall)
    copies[3].wait()

    def block(slot, p, t):
        points = ty[:, place(t)]
        norms = half_norms(points) * LOG2E
        for r in range(0, TILE, CHUNK):
            rows = slice(r, r + CHUNK)
            scores = (product(xs[p, rows, :], points) * LOG2E - norms) - both(tall[p, rows, :])
            costs[slot, rows, :] = scores
            terms = jnp.exp2(scores)
            mass[p, rows, :] += terms[:, LANES[0]] + terms[:, LANES[1]]

    for_blocks(codes, targets, block, 8)
    sums = lane_join(mass, jnp.sum)
    fill(out, jnp.log2(sums))

    @pl.when(jnp.min(sums) < SMALL)
    def _():
        top = tall
        top[...] = jnp.full_like(top, LOWEST)
        mass[...] = jnp.zeros_like(mass)

        def again(slot, p, t):
            one, two = costs[slot, :, LANES[0]], costs[slot, :, LANES[1]]
            old = top[p]
            new = jnp.maximum(old, jnp.maximum(one, two))
            top[p] = new
            mass[p] = mass[p] * jnp.exp2(old - new) + (jnp.exp2(one - new) + jnp.exp2(two - new))

        for_blocks(codes, targets, again, 1)
        lses = []
        for p in range(tiles):
            for h in range(2):
                tops, masses = top[p, LANES[h], :].T, mass[p, LANES[h], :].T
                peak = jnp.max(tops, axis=0, keepdims=True)
                lses.append(peak + jnp.log2(jnp.sum(masses * jnp.exp2(tops - peak), axis=0, keepdims=True)))
        fill(out, jnp.concatenate(lses, axis=0))


def both(tall):
    return jnp.concatenate([tall, tall], axis=1)


def col_first_kernel(log_ns, held_codes, costs, parts, f, out, peaks, terms, peak, total, tall, codes, sem):
    blocks = Codes(held_codes, codes, sem)
    rows = -log_ns - lse_of(parts_of(parts))
    f[...] = rows
    peak[...] = jnp.full_like(peak, LOWEST)
    total[...] = jnp.zeros_like(total)
    spread_tiles(rows, tall)

    def block(slot, p, t):
        scores = costs[slot] + both(tall[p])
        old = peak[t]
        new = jnp.maximum(old, jnp.max(scores, axis=0, keepdims=True))
        part = jnp.exp2(scores - new)
        terms[slot] = part
        peaks[slot] = new
        peak[t] = new
        total[t] = total[t] * jnp.exp2(old - new) + jnp.sum(part, axis=0, keepdims=True)

    for_blocks(blocks.ready(), out.shape[0], block, 8)
    masses = total[...]
    out[...] = jnp.where(masses > 0.0, peak[...] + jnp.log2(masses), LOWEST)


def row_kernel(first, held_codes, terms, b, given, out, *refs):
    made, _, acc, codes, sem = refs if first else (None, *refs)
    blocks = Codes(held_codes, codes, sem)
    acc[...] = jnp.zeros_like(acc)

    def block(slot, p, t):
        if first:
            factor = jnp.exp2(given[slot] + (b[t] + SHIFT))
            made[slot] = factor
        else:
            factor = given[slot] * b[t]
        for r in range(0, TILE, CHUNK):
            rows = slice(r, r + CHUNK)
            acc[p, rows, :] += (
                terms[slot, rows, LANES[0]] * factor[:, LANES[0]] + terms[slot, rows, LANES[1]] * factor[:, LANES[1]]
            )

    for_blocks(blocks.ready(), b.shape[0], block)
    fill(out, lane_join(acc, jnp.sum))


def col_kernel(ns, last, held_codes, terms, parts, factors, *refs):
    first, out, f, _, acc, tall, codes, sem = refs if last else (None, refs[0], None, *refs[1:])
    blocks = Codes(held_codes, codes, sem)
    a = 1.0 / (ns * total_of(parts_of(parts)))
    spread_tiles(a, tall)
    if last:
        f[...] = (first[...] + (jnp.log2(a) + SHIFT)) * LN2
    acc[...] = jnp.zeros_like(acc)

    def block(slot, p, t):
        sums = [[None] * 2, [None] * 2]
        for r in range(0, TILE, 8):
            factor = tall[p, r : r + 8, :]
            for h in range(2):
                term = terms[slot, r : r + 8, LANES[h]] * factor
                chain = (r // 8) % 2
                sums[h][chain] = term if sums[h][chain] is None else sums[h][chain] + term
        for h in range(2):
            acc[t, :, LANES[h]] += (sums[h][0] + sums[h][1]) * factors[slot, :, LANES[h]]

    for_blocks(blocks.ready(), out.shape[0], block)
    out[...] = jnp.sum(acc[...], axis=1, keepdims=True)


def join_first_kernel(log_nt, parts, g, out):
    g[...] = -log_nt - lse_of(parts_of(parts))
    fill(out, g[...])


def join_kernel(nt, parts, out):
    fill(out, 1.0 / (nt * total_of(parts_of(parts))))


def join_last_kernel(log_nt, parts, g, out):
    fill(out, (g[...] + (-log_nt - jnp.log2(total_of(parts_of(parts))))) * LN2)


def trade_tgt(pieces):
    order = [x * 2 + core for core in range(2) for x in range(4)]
    return lax.all_to_all(pieces, "tgt", 0, 0, axis_index_groups=[order])


def trade_src(pieces):
    order = [y * 8 + z for z in (0, 4, 2, 6, 1, 5, 3, 7) for y in (0, 2, 1, 3)]
    return lax.all_to_all(pieces, "src", 0, 0, axis_index_groups=[order])


def iterate(x, y, lists, counts, ns, nt, n_src, n_tgt, trade_tgt, trade_src):
    st, tt = x.shape[0] // TILE, y.shape[0] // TILE
    shape = (2 * st, HALF)
    share = (2 * tt // n_src, HALF)
    plain = lambda *shape: jax.ShapeDtypeStruct(shape, jnp.float32)
    scratch = lambda *shape: pltpu.VMEM(shape, jnp.float32)
    row, rows, col, cell, cells = like(shape), like((n_tgt, *shape)), like((tt, 1, TILE)), like(share), like((n_src, *share))
    length = (st * KLOC // HALF + 1) * HALF
    codes = jax.ShapeDtypeStruct((length,), jnp.int32)
    fetch = (pltpu.SMEM((length,), jnp.int32), pltpu.SemaphoreType.DMA((1,)))
    tall, stats = scratch(st, TILE, HALF), scratch(tt, 1, TILE)
    log_ns, log_nt = math.log2(ns), math.log2(nt)
    pieces = lambda v: trade_src(v.reshape((n_src, *share)))
    whole = lambda v: trade_src(v).reshape(tt, 1, TILE)

    blocks = like((st * KLOC, TILE, TILE))
    codes, lse, costs = call(
        row_first_kernel,
        (codes, rows, blocks),
        "svv",
        "hhhh",
        (lists.T, counts, x.T, y.T),
        (
            pltpu.VMEM((E, st * TILE), jnp.bfloat16),
            pltpu.VMEM((E, tt * TILE), jnp.bfloat16),
            pltpu.SMEM((KLOC, st), jnp.int32),
            pltpu.SMEM((st,), jnp.int32),
            pltpu.VMEM((st, TILE, E), jnp.bfloat16),
            tall,
            tall,
            pltpu.SemaphoreType.DMA((4,)),
        ),
        "row_first",
    )
    each = like((st * KLOC, 1, TILE))
    first, lse, peaks, terms = call(
        functools.partial(col_first_kernel, log_ns), (row, col, each, blocks), "vvvv", "vvv", (codes, costs, trade_tgt(lse)),
        (stats, stats, tall, *fetch), "col_first",
    )
    g, share_g = call(functools.partial(join_first_kernel, log_nt), (cell, cells), "vv", "v", (pieces(lse),), (), "join")
    mass, factors, terms = call(
        functools.partial(row_kernel, True), (rows, each), "vv", "vkvv", (codes, terms, whole(share_g), peaks),
        (tall, *fetch), "row_second",
    )
    for iteration in range(1, ITERS):
        last = iteration == ITERS - 1
        mass, *f, terms = call(
            functools.partial(col_kernel, ns, last), (col, plain(*shape)) if last else (col,), "vv" if last else "v",
            "vkvvv" if last else "vkvv", (codes, terms, trade_tgt(mass), factors) + ((first,) if last else ()),
            (scratch(tt, 8, TILE), tall, *fetch), "col",
        )
        if last:
            break
        (b,) = call(functools.partial(join_kernel, nt), (cells,), "v", "v", (pieces(mass),), (), "join")
        mass, terms = call(
            functools.partial(row_kernel, False), (rows,), "v", "vkvv", (codes, terms, whole(b), factors),
            (tall, *fetch), "row",
        )
    (share_g,) = call(functools.partial(join_last_kernel, log_nt), (cells,), "v", "vv", (pieces(mass), g), (), "join")
    return f[0].reshape(-1), trade_src(share_g).reshape(-1)


def local(source_points, target_points, tile_lists, tile_counts):
    n_src, n_tgt = lax.axis_size("src"), lax.axis_size("tgt")
    ns, nt = source_points.shape[0] * n_src, target_points.shape[0] * n_tgt
    return iterate(
        source_points, target_points, tile_lists[:, 0, :], tile_counts[:, 0], ns, nt, n_src, n_tgt, trade_tgt, trade_src
    )


def solution(mesh):
    in_specs = (P("src", None), P("tgt", None), P("src", "tgt", None), P("src", "tgt"))
    out_specs = (P("src"), P("tgt"))
    return jax.shard_map(local, mesh=mesh, in_specs=in_specs, out_specs=out_specs, check_vma=False)
```

```python
import functools
import math

import jax
import jax.numpy as jnp
from jax import lax
from jax.experimental import pallas as pl
from jax.experimental.pallas import tpu as pltpu
from jax.sharding import PartitionSpec as P

TILE = 256
HALF = 128
E = 64
KLOC = 4
ITERS = 4
LOWEST = -1e30
SHIFT = 32.0
LOG2E = math.log2(math.e)
LN2 = math.log(2.0)
SMALL = 2.0**-60
CHUNK = 128
LANES = (slice(0, HALF), slice(HALF, TILE))
VMEM_LIMIT = 12 * 1024 * 1024
RESIDENT = True


def held(x, space):
    return pltpu.with_memory_space_constraint(x, space) if RESIDENT else x


def like(shape, dtype=jnp.float32):
    return pltpu.VMEM(shape, dtype) if RESIDENT else jax.ShapeDtypeStruct(shape, dtype)


SPACE = {"s": pltpu.SMEM, "v": pltpu.VMEM, "k": pltpu.VMEM, "w": pltpu.VMEM, "a": pl.ANY, "h": pltpu.HBM}


def call(kernel, outs, out_specs, specs, args, scratch=(), name=None):
    specs_of = lambda letters: [pl.BlockSpec(memory_space=SPACE[s]) for s in letters]
    args = [held(arg, SPACE[spec]) if spec in "vkwh" else arg for spec, arg in zip(specs, args, strict=True)]
    keep = max(specs.find("k"), specs.find("w"))
    if keep >= 0:
        outs, out_specs = (*outs, like(args[keep].shape, args[keep].dtype)), out_specs + ("a" if "k" in specs else "v")
    return pl.pallas_call(
        kernel,
        out_shape=tuple(outs),
        in_specs=specs_of(specs),
        out_specs=tuple(specs_of(out_specs)),
        scratch_shapes=list(scratch),
        input_output_aliases={keep: len(outs) - 1} if keep >= 0 else {},
        compiler_params=pltpu.CompilerParams(vmem_limit_bytes=VMEM_LIMIT),
        name=name,
    )(*args)


class Codes:
    def __init__(self, held, codes, sem):
        self.copy = pltpu.make_async_copy(held, codes, sem.at[0])
        self.copy.start()
        self.codes = codes

    def ready(self):
        self.copy.wait()
        return self.codes


def for_blocks(codes, tiles, block, unroll=4):
    count = codes[codes.shape[0] - 1]

    def one(i):
        slot = lax.div(codes[i], tiles)
        block(slot, lax.div(slot, KLOC), codes[i] - slot * tiles)

    def several(i, _):
        for j in range(unroll):
            one(i * unroll + j)
        return 0

    def single(i, _):
        one(i)
        return 0

    groups = lax.div(count, unroll)
    lax.fori_loop(0, groups, several, 0)
    lax.fori_loop(groups * unroll, count, single, 0)


def place(t):
    return pl.ds(pl.multiple_of(t * TILE, TILE), TILE)


def spread_tiles(rows, tall):
    for p in range(tall.shape[0]):
        for h in range(2):
            row = rows[2 * p + h : 2 * p + h + 1, :]
            tall[p, LANES[h], :] = jnp.broadcast_to(row, (HALF, HALF)).T


def lane_join(tall, join):
    rows = []
    for p in range(tall.shape[0]):
        for h in range(2):
            rows.append(join(tall[p, LANES[h], :].T, axis=0, keepdims=True))
    return jnp.concatenate(rows, axis=0)


def fill(out, value):
    for d in range(out.shape[0]):
        out[d] = value


def total_of(parts):
    return functools.reduce(jnp.add, parts)


def parts_of(ref):
    return [ref[d] for d in range(ref.shape[0])]


def lse_of(parts):
    top = functools.reduce(jnp.maximum, parts)
    return top + jnp.log2(total_of([jnp.exp2(part - top) for part in parts]))


def product(a, b):
    return jnp.dot(a, b, preferred_element_type=jnp.float32)


def half_norms(points):
    wide = points.astype(jnp.float32)
    return 0.5 * jnp.sum(wide * wide, axis=0, keepdims=True)


def lane_rows(row):
    return jnp.concatenate([row[:, i : i + HALF] for i in range(0, row.shape[1], HALF)], axis=0)


def row_first_kernel(lists_in, counts_in, x, y, codes, out, costs, tx, ty, lists, counts, xs, tall, mass, sems):
    tiles, targets = xs.shape[0], ty.shape[1] // TILE
    pairs = ((lists_in, lists), (counts_in, counts), (x, tx), (y, ty))
    copies = [pltpu.make_async_copy(*pair, sems.at[i]) for i, pair in enumerate(pairs)]
    for copy in copies:
        copy.start()
    mass[...] = jnp.zeros_like(mass)
    copies[0].wait()
    copies[1].wait()

    def listed(p, n):
        for k in range(KLOC):
            codes[n + k] = (p * KLOC + k) * targets + lists[k, p]
        return n + counts[p]

    codes[codes.shape[0] - 1] = lax.fori_loop(0, tiles, listed, 0)
    copies[2].wait()
    norms = []
    for p in range(tiles):
        points = tx[:, p * TILE : (p + 1) * TILE]
        norms.append(lane_rows(half_norms(points)))
        xs[p] = points.astype(jnp.float32).T.astype(jnp.bfloat16)
    spread_tiles(jnp.concatenate(norms, axis=0) * LOG2E, tall)
    copies[3].wait()

    def block(slot, p, t):
        points = ty[:, place(t)]
        norms = half_norms(points) * LOG2E
        for r in range(0, TILE, CHUNK):
            rows = slice(r, r + CHUNK)
            scores = (product(xs[p, rows, :], points) * LOG2E - norms) - both(tall[p, rows, :])
            costs[slot, rows, :] = scores
            terms = jnp.exp2(scores)
            mass[p, rows, :] += terms[:, LANES[0]] + terms[:, LANES[1]]

    for_blocks(codes, targets, block, 8)
    sums = lane_join(mass, jnp.sum)
    fill(out, jnp.log2(sums))

    @pl.when(jnp.min(sums) < SMALL)
    def _():
        top = tall
        top[...] = jnp.full_like(top, LOWEST)
        mass[...] = jnp.zeros_like(mass)

        def again(slot, p, t):
            one, two = costs[slot, :, LANES[0]], costs[slot, :, LANES[1]]
            old = top[p]
            new = jnp.maximum(old, jnp.maximum(one, two))
            top[p] = new
            mass[p] = mass[p] * jnp.exp2(old - new) + (jnp.exp2(one - new) + jnp.exp2(two - new))

        for_blocks(codes, targets, again, 1)
        lses = []
        for p in range(tiles):
            for h in range(2):
                tops, masses = top[p, LANES[h], :].T, mass[p, LANES[h], :].T
                peak = jnp.max(tops, axis=0, keepdims=True)
                lses.append(peak + jnp.log2(jnp.sum(masses * jnp.exp2(tops - peak), axis=0, keepdims=True)))
        fill(out, jnp.concatenate(lses, axis=0))


def both(tall):
    return jnp.concatenate([tall, tall], axis=1)


def col_first_kernel(log_ns, held_codes, costs, parts, f, out, peaks, terms, peak, total, tall, codes, sem):
    blocks = Codes(held_codes, codes, sem)
    rows = -log_ns - lse_of(parts_of(parts))
    f[...] = rows
    peak[...] = jnp.full_like(peak, LOWEST)
    total[...] = jnp.zeros_like(total)
    spread_tiles(rows, tall)

    def block(slot, p, t):
        scores = costs[slot] + both(tall[p])
        old = peak[t]
        new = jnp.maximum(old, jnp.max(scores, axis=0, keepdims=True))
        part = jnp.exp2(scores - new)
        terms[slot] = part
        peaks[slot] = new
        peak[t] = new
        total[t] = total[t] * jnp.exp2(old - new) + jnp.sum(part, axis=0, keepdims=True)

    for_blocks(blocks.ready(), out.shape[0], block, 8)
    masses = total[...]
    out[...] = jnp.where(masses > 0.0, peak[...] + jnp.log2(masses), LOWEST)


def row_kernel(first, held_codes, terms, b, given, out, *refs):
    made, _, acc, codes, sem = refs if first else (None, *refs)
    blocks = Codes(held_codes, codes, sem)
    acc[...] = jnp.zeros_like(acc)

    def block(slot, p, t):
        if first:
            factor = jnp.exp2(given[slot] + (b[t] + SHIFT))
            made[slot] = factor
        else:
            factor = given[slot] * b[t]
        for r in range(0, TILE, CHUNK):
            rows = slice(r, r + CHUNK)
            acc[p, rows, :] += (
                terms[slot, rows, LANES[0]] * factor[:, LANES[0]] + terms[slot, rows, LANES[1]] * factor[:, LANES[1]]
            )

    for_blocks(blocks.ready(), b.shape[0], block)
    fill(out, lane_join(acc, jnp.sum))


def col_kernel(ns, last, held_codes, terms, parts, factors, *refs):
    first, out, f, _, acc, tall, codes, sem = refs if last else (None, refs[0], None, *refs[1:])
    blocks = Codes(held_codes, codes, sem)
    a = 1.0 / (ns * total_of(parts_of(parts)))
    spread_tiles(a, tall)
    if last:
        f[...] = (first[...] + (jnp.log2(a) + SHIFT)) * LN2
    acc[...] = jnp.zeros_like(acc)

    def block(slot, p, t):
        sums = [[None] * 2, [None] * 2]
        for r in range(0, TILE, 8):
            factor = tall[p, r : r + 8, :]
            for h in range(2):
                term = terms[slot, r : r + 8, LANES[h]] * factor
                chain = (r // 8) % 2
                sums[h][chain] = term if sums[h][chain] is None else sums[h][chain] + term
        for h in range(2):
            acc[t, :, LANES[h]] += (sums[h][0] + sums[h][1]) * factors[slot, :, LANES[h]]

    for_blocks(blocks.ready(), out.shape[0], block)
    out[...] = jnp.sum(acc[...], axis=1, keepdims=True)


def join_first_kernel(log_nt, parts, g, out):
    g[...] = -log_nt - lse_of(parts_of(parts))
    fill(out, g[...])


def join_kernel(nt, parts, out):
    fill(out, 1.0 / (nt * total_of(parts_of(parts))))


def join_last_kernel(log_nt, parts, g, out):
    fill(out, (g[...] + (-log_nt - jnp.log2(total_of(parts_of(parts))))) * LN2)


def trade_tgt(pieces):
    order = [x * 2 + core for core in range(2) for x in range(4)]
    return lax.all_to_all(pieces, "tgt", 0, 0, axis_index_groups=[order])


def trade_src(pieces):
    order = [y * 8 + z for z in (0, 4, 2, 6, 1, 5, 3, 7) for y in (0, 2, 1, 3)]
    return lax.all_to_all(pieces, "src", 0, 0, axis_index_groups=[order])


def iterate(x, y, lists, counts, ns, nt, n_src, n_tgt, trade_tgt, trade_src):
    st, tt = x.shape[0] // TILE, y.shape[0] // TILE
    shape = (2 * st, HALF)
    share = (2 * tt // n_src, HALF)
    plain = lambda *shape: jax.ShapeDtypeStruct(shape, jnp.float32)
    scratch = lambda *shape: pltpu.VMEM(shape, jnp.float32)
    row, rows, col, cell, cells = like(shape), like((n_tgt, *shape)), like((tt, 1, TILE)), like(share), like((n_src, *share))
    length = (st * KLOC // HALF + 1) * HALF
    codes = jax.ShapeDtypeStruct((length,), jnp.int32)
    fetch = (pltpu.SMEM((length,), jnp.int32), pltpu.SemaphoreType.DMA((1,)))
    tall, stats = scratch(st, TILE, HALF), scratch(tt, 1, TILE)
    log_ns, log_nt = math.log2(ns), math.log2(nt)
    pieces = lambda v: trade_src(v.reshape((n_src, *share)))
    whole = lambda v: trade_src(v).reshape(tt, 1, TILE)

    blocks = like((st * KLOC, TILE, TILE))
    codes, lse, costs = call(
        row_first_kernel,
        (codes, rows, blocks),
        "svv",
        "hhhh",
        (lists.T, counts, x.T, y.T),
        (
            pltpu.VMEM((E, st * TILE), jnp.bfloat16),
            pltpu.VMEM((E, tt * TILE), jnp.bfloat16),
            pltpu.SMEM((KLOC, st), jnp.int32),
            pltpu.SMEM((st,), jnp.int32),
            pltpu.VMEM((st, TILE, E), jnp.bfloat16),
            tall,
            tall,
            pltpu.SemaphoreType.DMA((4,)),
        ),
        "row_first",
    )
    each = like((st * KLOC, 1, TILE))
    first, lse, peaks, terms = call(
        functools.partial(col_first_kernel, log_ns), (row, col, each, blocks), "vvvv", "vvv", (codes, costs, trade_tgt(lse)),
        (stats, stats, tall, *fetch), "col_first",
    )
    g, share_g = call(functools.partial(join_first_kernel, log_nt), (cell, cells), "vv", "v", (pieces(lse),), (), "join")
    mass, factors, terms = call(
        functools.partial(row_kernel, True), (rows, each), "vv", "vkvv", (codes, terms, whole(share_g), peaks),
        (tall, *fetch), "row_second",
    )
    for iteration in range(1, ITERS):
        last = iteration == ITERS - 1
        mass, *f, terms = call(
            functools.partial(col_kernel, ns, last), (col, plain(*shape)) if last else (col,), "vv" if last else "v",
            "vkvvv" if last else "vkvv", (codes, terms, trade_tgt(mass), factors) + ((first,) if last else ()),
            (scratch(tt, 8, TILE), tall, *fetch), "col",
        )
        if last:
            break
        (b,) = call(functools.partial(join_kernel, nt), (cells,), "v", "v", (pieces(mass),), (), "join")
        mass, terms = call(
            functools.partial(row_kernel, False), (rows,), "v", "vkvv", (codes, terms, whole(b), factors),
            (tall, *fetch), "row",
        )
    (share_g,) = call(functools.partial(join_last_kernel, log_nt), (cells,), "v", "vv", (pieces(mass), g), (), "join")
    return f[0].reshape(-1), trade_src(share_g).reshape(-1)


def local(source_points, target_points, tile_lists, tile_counts):
    n_src, n_tgt = lax.axis_size("src"), lax.axis_size("tgt")
    ns, nt = source_points.shape[0] * n_src, target_points.shape[0] * n_tgt
    return iterate(
        source_points, target_points, tile_lists[:, 0, :], tile_counts[:, 0], ns, nt, n_src, n_tgt, trade_tgt, trade_src
    )


def solution(mesh):
    in_specs = (P("src", None), P("tgt", None), P("src", "tgt", None), P("src", "tgt"))
    out_specs = (P("src"), P("tgt"))
    return jax.shard_map(local, mesh=mesh, in_specs=in_specs, out_specs=out_specs, check_vma=False)
```
